256 devices in a mesh: seq: 64 (over x, z_lo, y), tp: 4 (over z_hi, core).
Axes of the slice: x: 4, y: 4, z: 8 (z_hi: 2, z_lo: 4; z = z_hi * 4 + z_lo), core: 2. Of those that a mesh axis runs over, the one named last changes fastest.
Arguments:
- latents: float32 [256, 256, 1152], P('tp', 'seq'), may hold values from -100 to 100
- time_embed: float32 [256, 1152], P('seq'), may hold values from -3 to 3
- modulation: float32 [3, 3, 1152], replicated, may hold values from -2 to 2
- qkv_weight: bfloat16 [2, 1152, 3, 1152], P(None, None, None, 'tp'), may hold values from -6 to 6
- out_weight: bfloat16 [2, 1152, 1152], P(None, 'tp'), may hold values from -0.1875 to 0.1875
- mlp_in_weight: bfloat16 [1152, 4608], P(None, 'tp'), may hold values from -0.1875 to 0.1875
- mlp_out_weight: bfloat16 [4608, 1152], P('tp'), may hold values from -0.09375 to 0.09375
Outputs:
- result: float32 [256, 256, 1152], P('tp', 'seq')
The draws below stay inside these ranges and needn't reach their ends.
All inputs are finite; a program needn't handle non-finite values.
Results may differ from the reference program's by a relative error of at most 0.0045.
Values may be sent and summed in bfloat16 or wider, within the bound.
No kernel may reach another device: no remote copies, remote signals or barrier semaphores. Data moves between devices by JAX's collectives and lax.ppermute only.
A program may use at most 128 MiB of HBM per device.

```python
import math
import jax
import jax.numpy as jnp
from jax import lax

D = 1152
HEADS = 16
HD = 72
FF = 4608
P_SIZE = 256
FRAMES = 256
N_TP = 4


def draw_latents(key, part):
    key = jax.random.fold_in(key, 11)
    column_key, row_key, basis_key = jax.random.split(key, 3)
    column_scale = jnp.exp(jax.random.uniform(column_key, (D,), jnp.float32, math.log(0.5), math.log(2.0)))
    row_scale = jnp.exp(jax.random.uniform(row_key, (P_SIZE, FRAMES, 1), jnp.float32, math.log(0.3), math.log(3.0)))
    basis = jax.random.normal(basis_key, (P_SIZE, FRAMES, D), jnp.float32)
    return basis * row_scale * column_scale


def draw_qkv_weight(key, part):
    key = jax.random.fold_in(key, 23)
    basis_key = jax.random.fold_in(key, 0)
    basis = jax.random.normal(basis_key, (2, D, 3, D), jnp.float32) * D ** (-0.5)
    return basis.astype(jnp.bfloat16)


def block_levels(key, shape, pieces, smallest, top_value):
    def one(position, shards_of):
        draws = jax.random.uniform(jax.random.fold_in(jax.random.fold_in(key, 6), position), (shards_of,), jnp.float32, smallest / len(pieces), top_value / len(pieces))
        return jnp.repeat(jnp.exp(draws), shape[position] // shards_of).reshape((-1,) + (1,) * (len(shape) - position - 1))

    factor_of = one(*pieces[0])
    for cut in pieces[1:]:
        factor_of = factor_of * one(*cut)
    return factor_of


def bell_draw(rng, dims, width, bound, pieces=(), kind=jnp.bfloat16):
    entries = width * jax.random.normal(rng, dims, jnp.float32)
    if pieces:
        entries = entries * block_levels(rng, dims, pieces, -0.22, 0.18)
    return jnp.clip(entries, -bound, bound).astype(kind)


def setup_inputs(seed: int = 0) -> dict:
    arg_keys = jax.random.split(jax.random.key(seed), 8)
    latents = draw_latents(jax.random.fold_in(arg_keys[7], 71), 0)
    time_embed = bell_draw(arg_keys[1], (FRAMES, D), 0.5, 3.0, ((0, 64),), jnp.float32)
    modulation = bell_draw(arg_keys[2], (3, 3, D), 0.3, 2.0, (), jnp.float32)
    qkv_weight = draw_qkv_weight(jax.random.fold_in(arg_keys[7], 71), 0)
    out_weight = bell_draw(arg_keys[4], (2, D, D), D ** -0.5, 0.1875, ((1, 4),))
    mlp_in_weight = bell_draw(arg_keys[5], (D, FF), D ** -0.5, 0.1875, ((1, 4),))
    mlp_out_weight = bell_draw(arg_keys[6], (FF, D), FF ** -0.5, 0.09375, ((0, 4),))
    return dict(latents=latents, time_embed=time_embed, modulation=modulation, qkv_weight=qkv_weight, out_weight=out_weight, mlp_in_weight=mlp_in_weight, mlp_out_weight=mlp_out_weight)


def modulate(hidden, gains):
    average = lax.optimization_barrier(jnp.mean(hidden, axis=-1, keepdims=True))
    centred = hidden - average
    spread = lax.optimization_barrier(jnp.mean(centred * centred, axis=-1, keepdims=True))
    return (centred * lax.rsqrt(spread + 1e-06) * (1.0 + gains[1]) + gains[0]).astype(jnp.bfloat16)

def sublayer(section, qkv_flat, out_groups, gains):
    count_items, length = (section.shape[0], section.shape[1])
    normed = modulate(section, gains).reshape(count_items * length, D)
    packed = jnp.dot(normed, qkv_flat, preferred_element_type=jnp.float32)
    packed = packed.reshape(count_items, length, 3, HEADS, HD)
    queries = packed[:, :, 0]
    key_rows = packed[:, :, 1]
    values = packed[:, :, 2].astype(jnp.bfloat16)
    scores = jnp.einsum('ilhd,imhd->ihlm', queries, key_rows, precision=lax.Precision.HIGHEST) * (1.0 / math.sqrt(HD))
    highest = lax.optimization_barrier(jnp.max(scores, axis=-1, keepdims=True))
    exponent = jnp.exp(scores - highest)
    weights = (exponent / lax.optimization_barrier(jnp.sum(exponent, axis=-1, keepdims=True))).astype(jnp.bfloat16)
    mixed = jnp.einsum('ihlm,imhd->ilhd', weights.astype(jnp.float32), values.astype(jnp.float32)).astype(jnp.bfloat16)
    grouped = mixed.reshape(count_items * length, N_TP, D // N_TP).astype(jnp.float32)
    partials = jnp.einsum('rgc,gcd->rgd', grouped, out_groups.astype(jnp.float32)).astype(jnp.bfloat16)
    projected = lax.optimization_barrier(jnp.sum(partials.astype(jnp.float32), axis=1))
    return section + gains[2] * projected.reshape(section.shape)

def feed_forward(section, w_in, out_groups, gains):
    normed = modulate(section, gains).reshape(-1, D)
    inner = jax.nn.gelu(jnp.dot(normed, w_in, preferred_element_type=jnp.float32), approximate=True).astype(jnp.bfloat16)
    grouped = inner.reshape(-1, N_TP, FF // N_TP).astype(jnp.float32)
    partials = jnp.einsum('rgc,gcd->rgd', grouped, out_groups.astype(jnp.float32)).astype(jnp.bfloat16)
    projected = lax.optimization_barrier(jnp.sum(partials.astype(jnp.float32), axis=1))
    return section + gains[2] * projected.reshape(section.shape)

def reference(latents, time_embed, modulation, qkv_weight, out_weight, mlp_in_weight, mlp_out_weight):
    span_frames = math.gcd(FRAMES, 8)
    span_positions = math.gcd(P_SIZE, 8)
    flat_spatial = qkv_weight[0].reshape(D, 3 * D)
    flat_temporal = qkv_weight[1].reshape(D, 3 * D)
    groups_spatial = out_weight[0].reshape(N_TP, D // N_TP, D)
    groups_temporal = out_weight[1].reshape(N_TP, D // N_TP, D)
    groups_mlp = mlp_out_weight.reshape(N_TP, FF // N_TP, D)
    frame_major = jnp.swapaxes(latents, 0, 1).reshape(FRAMES // span_frames, span_frames, P_SIZE, D)
    embed_blocks = time_embed.reshape(FRAMES // span_frames, span_frames, D)

    def spatial(inputs_pair):
        section, embedding = inputs_pair
        return sublayer(section, flat_spatial, groups_spatial, modulation[0]) + embedding[:, None, :]
    middle = lax.map(spatial, (frame_major, embed_blocks)).reshape(FRAMES, P_SIZE, D)
    position_major = jnp.swapaxes(middle, 0, 1).reshape(P_SIZE // span_positions, span_positions, FRAMES, D)

    def temporal(section):
        after = sublayer(section, flat_temporal, groups_temporal, modulation[1])
        return feed_forward(after, mlp_in_weight, groups_mlp, modulation[2])
    return lax.map(temporal, position_major).reshape(P_SIZE, FRAMES, D)
```

```python
import math

import jax
import jax.numpy as jnp
from jax import lax
from jax.experimental import pallas as pl
from jax.experimental.pallas import tpu as pltpu
from jax.sharding import PartitionSpec as P

HD = 72
BF = jnp.bfloat16
F32 = jnp.float32
PLANE = [[x * 16 + z * 4 + y for x in range(4) for y in range(4)] for z in range(4)]
SWAPS = {d: [(t, t ^ d) for t in range(4)] for d in (1, 2, 3)}


def modulate(hidden, gains):
    average = jnp.mean(hidden, axis=-1, keepdims=True)
    centred = hidden - average
    spread = jnp.mean(centred * centred, axis=-1, keepdims=True)
    return (centred * lax.rsqrt(spread + 1e-06) * (1.0 + gains[1]) + gains[0]).astype(BF)


def dot(a, b, ca, cb):
    return lax.dot_general(a, b, (((ca,), (cb,)), ((), ())), preferred_element_type=F32)


def attend_kernel(x_ref, w0, w1, w2, w3, out_ref, held, sems):
    sources = (w0, w1, w2, w3)
    heads = 4
    width = heads * HD
    for k in range(4):
        pltpu.make_async_copy(sources[k], held.at[k], sems.at[k]).start()
    x = x_ref[...]

    def shard(k):
        pltpu.make_async_copy(sources[k], held.at[k], sems.at[k]).wait()
        packed = dot(held[k, : 3 * width, :], x, 1, 1)
        mixed = []
        for h in range(heads):
            q = packed[h * HD : (h + 1) * HD] * (math.log2(math.e) / math.sqrt(HD))
            kk = packed[width + h * HD : width + (h + 1) * HD]
            v = packed[2 * width + h * HD : 2 * width + (h + 1) * HD].astype(BF)
            qh = q.astype(BF).astype(F32)
            kh = kk.astype(BF).astype(F32)
            left = jnp.concatenate([kh, kh, kk - kh], axis=0).astype(BF)
            right = jnp.concatenate([qh, q - qh, qh], axis=0).astype(BF)
            scores = dot(left, right, 0, 0)
            top = jnp.max(scores, axis=0, keepdims=True)
            weights = jnp.exp2(scores - top)
            total = jnp.sum(weights, axis=0, keepdims=True)
            mixed.append(dot(v, weights.astype(BF), 1, 0) / total)
        rows = jnp.concatenate(mixed, axis=0).astype(BF)
        return dot(rows, held[k, 3 * width :, :], 0, 0)

    total = shard(0)
    for k in range(1, 4):
        total = total + shard(k)
    out_ref[...] = total.astype(out_ref.dtype)


def attend(x, shards):
    rows, width = x.shape
    return pl.pallas_call(
        attend_kernel,
        out_shape=jax.ShapeDtypeStruct((rows, width), BF),
        in_specs=[pl.BlockSpec(memory_space=pltpu.VMEM)] + [pl.BlockSpec(memory_space=pl.ANY)] * 4,
        out_specs=pl.BlockSpec(memory_space=pltpu.VMEM),
        scratch_shapes=[
            pltpu.VMEM((4, width, width), BF),
            pltpu.SemaphoreType.DMA((4,)),
        ],
        compiler_params=pltpu.CompilerParams(vmem_limit_bytes=48 * 2**20),
        cost_estimate=pl.CostEstimate(
            flops=2 * rows * width * width * 4, bytes_accessed=8 * width * width, transcendentals=0
        ),
    )(x, *shards)


def mlp_kernel(x_ref, a0, a1, a2, a3, b0, b1, b2, b3, out_ref, held, sems):
    sources = (a0, b0, a1, b1, a2, b2, a3, b3)
    for k in range(8):
        pltpu.make_async_copy(sources[k], held.at[k], sems.at[k]).start()
    x = x_ref[...]
    total = None
    for k in range(4):
        pltpu.make_async_copy(sources[2 * k], held.at[2 * k], sems.at[2 * k]).wait()
        v = dot(x, held[2 * k], 1, 0)
        inner = 0.5 * v * (1.0 + jnp.tanh(math.sqrt(2.0 / math.pi) * (v + 0.044715 * (v * v * v))))
        pltpu.make_async_copy(sources[2 * k + 1], held.at[2 * k + 1], sems.at[2 * k + 1]).wait()
        part = dot(inner.astype(BF), held[2 * k + 1], 1, 0)
        total = part if total is None else total + part
    out_ref[...] = total


def mlp(x, w_in, w_out):
    rows, width = x.shape
    return pl.pallas_call(
        mlp_kernel,
        out_shape=jax.ShapeDtypeStruct((rows, width), F32),
        in_specs=[pl.BlockSpec(memory_space=pltpu.VMEM)] + [pl.BlockSpec(memory_space=pl.ANY)] * 8,
        out_specs=pl.BlockSpec(memory_space=pltpu.VMEM),
        scratch_shapes=[
            pltpu.VMEM((8, width, width), BF),
            pltpu.SemaphoreType.DMA((8,)),
        ],
        compiler_params=pltpu.CompilerParams(vmem_limit_bytes=48 * 2**20),
        cost_estimate=pl.CostEstimate(
            flops=2 * rows * width * width * 8, bytes_accessed=16 * width * width, transcendentals=0
        ),
    )(x, *w_in, *w_out)


def all_shards(own, place):
    piece_rows = own.shape[0] // 16
    piece = lax.dynamic_slice_in_dim(own, place * piece_rows, piece_rows, axis=0)
    piece = lax.ppermute(piece, "tp", SWAPS[2])
    far = lax.all_gather(piece, "seq", axis=0, tiled=True, axis_index_groups=PLANE)
    return own, lax.ppermute(own, "tp", SWAPS[1]), far, lax.ppermute(far, "tp", SWAPS[1])


def on_device(
    latents, time_embed, modulation, qkv_weight, out_weight, mlp_in_weight, mlp_out_weight
):
    width = latents.shape[2]
    seq = lax.axis_index("seq")
    tp = lax.axis_index("tp")
    place = (seq // 16) * 4 + seq % 4
    flat = qkv_weight.transpose(0, 2, 3, 1).reshape(2, -1, width)
    layers = [jnp.concatenate([flat[b], out_weight[b]], axis=0) for b in range(2)]
    spatial = all_shards(layers[0], place)
    temporal = all_shards(layers[1], place)
    w_in = all_shards(mlp_in_weight, place)
    w_out = all_shards(mlp_out_weight, place)

    normed = modulate(latents, modulation[0]).transpose(1, 0, 2)

    def frame(rows, d):
        return lax.dynamic_index_in_dim(rows, tp ^ d, axis=0, keepdims=False)

    parts = [frame(normed, 0)] + [lax.ppermute(frame(normed, d), "tp", SWAPS[d]) for d in (1, 2, 3)]
    projected = attend(jnp.concatenate(parts, axis=0), spatial).reshape(4, -1, width)
    back = [projected[0]] + [lax.ppermute(projected[d], "tp", SWAPS[d]) for d in (1, 2, 3)]
    odd = (tp & 1) == 1
    high = (tp & 2) == 2
    back = [jnp.where(odd, back[d ^ 1], back[d]) for d in range(4)]
    back = [jnp.where(high, back[d ^ 2], back[d]) for d in range(4)]
    projected = jnp.stack(back, axis=1).astype(F32)
    middle = latents + modulation[0, 2] * projected + time_embed[None]
    normed = modulate(middle, modulation[1])
    regrouped = lax.all_to_all(normed, "seq", split_axis=0, concat_axis=0, tiled=True)
    projected = attend(regrouped.reshape(-1, width), temporal).reshape(regrouped.shape)
    projected = lax.all_to_all(projected, "seq", split_axis=0, concat_axis=0, tiled=True)
    after_t = middle + modulation[1, 2] * projected.astype(F32)
    normed = modulate(after_t, modulation[2]).reshape(-1, width)
    projected = mlp(normed, w_in, w_out).reshape(after_t.shape)
    return after_t + modulation[2, 2] * projected


def solution(mesh):
    in_specs = (
        P("tp", "seq", None),
        P("seq", None),
        P(),
        P(None, None, None, "tp"),
        P(None, "tp", None),
        P(None, "tp"),
        P("tp", None),
    )
    out_specs = P("tp", "seq", None)
    return jax.shard_map(
        on_device, mesh=mesh, in_specs=in_specs, out_specs=out_specs, check_vma=False
    )
```

```python
import functools
import math

import jax
import jax.numpy as jnp
from jax import lax
from jax.experimental import pallas as pl
from jax.experimental.pallas import tpu as pltpu
from jax.sharding import PartitionSpec as P

HD = 72
BF = jnp.bfloat16
F32 = jnp.float32
PLANE = [[x * 16 + z * 4 + y for x in range(4) for y in range(4)] for z in range(4)]
SWAPS = {d: [(t, t ^ d) for t in range(4)] for d in (1, 2, 3)}


def modulate(hidden, gains):
    average = jnp.mean(hidden, axis=-1, keepdims=True)
    centred = hidden - average
    spread = jnp.mean(centred * centred, axis=-1, keepdims=True)
    return (centred * lax.rsqrt(spread + 1e-06) * (1.0 + gains[1]) + gains[0]).astype(BF)


def dot(a, b, ca, cb):
    return lax.dot_general(a, b, (((ca,), (cb,)), ((), ())), preferred_element_type=F32)


def attend_kernel(pieces, ready, layer, *refs):
    x_refs, refs = refs[:pieces], refs[pieces:]
    inits, refs = refs[:ready], refs[ready:]
    out_refs, (held, sems) = refs[-pieces - 2 : -2], refs[-2:]
    sources = refs[: -pieces - 2]
    heads = 4
    width = heads * HD
    length = 256
    plan = []
    if len(sources) == 4:
        for k in range(2):
            plan.append((sources[2 * k].at[layer], held.at[k, pl.ds(0, 3 * width)]))
            plan.append((sources[2 * k + 1].at[layer], held.at[k, pl.ds(3 * width, width)]))
    else:
        for k in range(2):
            plan.append((sources[k], held.at[k]))
    copies = [pltpu.make_async_copy(a, b, sems.at[i]) for i, (a, b) in enumerate(plan)]
    for copy in copies:
        copy.start()
    each = len(copies) // 2
    items = x_refs[0].shape[0]
    x = jnp.concatenate([ref[s] for s in range(items) for ref in x_refs], axis=0)

    def shard(k):
        for copy in copies[each * k : each * (k + 1)]:
            copy.wait()
        packed = dot(held[k, : 3 * width, :], x, 1, 1)
        columns = []
        for s in range(items):
            item = packed[:, s * length : (s + 1) * length]
            mixed = []
            for h in range(heads):
                q = item[h * HD : (h + 1) * HD] * (math.log2(math.e) / math.sqrt(HD))
                kk = item[width + h * HD : width + (h + 1) * HD]
                v = item[2 * width + h * HD : 2 * width + (h + 1) * HD].astype(BF)
                qh = q.astype(BF).astype(F32)
                kh = kk.astype(BF).astype(F32)
                left = jnp.concatenate([kh, kh, kk - kh], axis=0).astype(BF)
                right = jnp.concatenate([qh, q - qh, qh], axis=0).astype(BF)
                scores = dot(left, right, 0, 0)
                top = jnp.max(scores, axis=0, keepdims=True)
                weights = jnp.exp2(scores - top)
                total = jnp.sum(weights, axis=0, keepdims=True)
                mixed.append(dot(v, weights.astype(BF), 1, 0) / total)
            columns.append(jnp.concatenate(mixed, axis=0).astype(BF))
        return dot(jnp.concatenate(columns, axis=1), held[k, 3 * width :, :], 0, 0)

    total = shard(0) + shard(1)
    if ready:
        total = total + inits[0][0]
    total = total.astype(out_refs[0].dtype)
    part = length // pieces
    for s in range(items):
        for d in range(pieces):
            start = s * length + d * part
            out_refs[d][s] = total[start : start + part]


def attend(layer, parts, weights, inits=(), kind=BF):
    items, _, width = parts[0].shape
    rows = items * 256
    pieces = len(parts)
    return pl.pallas_call(
        functools.partial(attend_kernel, pieces, len(inits), layer),
        out_shape=[jax.ShapeDtypeStruct(part.shape, kind) for part in parts],
        in_specs=[pl.BlockSpec(memory_space=pltpu.VMEM)] * (pieces + len(inits))
        + [pl.BlockSpec(memory_space=pl.ANY)] * len(weights),
        out_specs=[pl.BlockSpec(memory_space=pltpu.VMEM)] * pieces,
        scratch_shapes=[
            pltpu.VMEM((2, width, width), BF),
            pltpu.SemaphoreType.DMA((len(weights),)),
        ],
        compiler_params=pltpu.CompilerParams(vmem_limit_bytes=48 * 2**20),
        cost_estimate=pl.CostEstimate(
            flops=6 * rows * width * width,
            bytes_accessed=4 * width * width,
            transcendentals=0,
        ),
    )(*parts, *inits, *weights)


def mlp_kernel(ready, count, x_ref, *refs):
    inits, refs = refs[:ready], refs[ready:]
    sources, (out_ref, held, sems) = refs[:count], refs[count:]
    width = x_ref.shape[1]
    blocks = []
    for ref in sources:
        for part in range(ref.shape[0] // width):
            blocks.append(ref.at[pl.ds(part * width, width)])
    copies = [pltpu.make_async_copy(b, held.at[i], sems.at[i]) for i, b in enumerate(blocks)]
    for copy in copies:
        copy.start()
    x = x_ref[...]
    total = inits[0][...] if ready else None
    for k in range(0, len(blocks), 2):
        copies[k].wait()
        v = dot(x, held[k], 1, 0)
        inner = 0.5 * v * (1.0 + jnp.tanh(math.sqrt(2.0 / math.pi) * (v + 0.044715 * (v * v * v))))
        copies[k + 1].wait()
        part = dot(inner.astype(BF), held[k + 1], 1, 0)
        total = part if total is None else total + part
    out_ref[...] = total


def mlp(x, weights, inits=()):
    rows, width = x.shape
    blocks = sum(w.shape[0] for w in weights) // width
    return pl.pallas_call(
        functools.partial(mlp_kernel, len(inits), len(weights)),
        out_shape=jax.ShapeDtypeStruct((rows, width), F32),
        in_specs=[pl.BlockSpec(memory_space=pltpu.VMEM)] * (1 + len(inits))
        + [pl.BlockSpec(memory_space=pl.ANY)] * len(weights),
        out_specs=pl.BlockSpec(memory_space=pltpu.VMEM),
        scratch_shapes=[
            pltpu.VMEM((blocks, width, width), BF),
            pltpu.SemaphoreType.DMA((blocks,)),
        ],
        compiler_params=pltpu.CompilerParams(vmem_limit_bytes=48 * 2**20),
        cost_estimate=pl.CostEstimate(
            flops=2 * rows * width * width * blocks,
            bytes_accessed=2 * blocks * width * width,
            transcendentals=0,
        ),
    )(x, *inits, *weights)


def swap(x, d):
    return lax.ppermute(x, "tp", SWAPS[d])


def gather(piece):
    return lax.all_gather(piece, "seq", axis=0, tiled=True, axis_index_groups=PLANE)


def no_work(*refs):
    del refs


def after(x, *others):
    return pl.pallas_call(
        no_work,
        out_shape=jax.ShapeDtypeStruct(x.shape, x.dtype),
        in_specs=[pl.BlockSpec(memory_space=pl.ANY)] * (1 + len(others)),
        out_specs=pl.BlockSpec(memory_space=pl.ANY),
        input_output_aliases={0: 0},
    )(x, *others)


def on_device(
    latents, time_embed, modulation, qkv_weight, out_weight, mlp_in_weight, mlp_out_weight
):
    width = latents.shape[2]
    seq = lax.axis_index("seq")
    tp = lax.axis_index("tp")
    place = (seq // 16) * 4 + seq % 4
    core = tp % 2

    qkv = qkv_weight.transpose(0, 2, 3, 1).reshape(2, -1, width)
    other_qkv = swap(qkv, 1)
    other_out = swap(out_weight, 1)
    near = (qkv, out_weight, other_qkv, other_out)

    normed = modulate(latents, modulation[0]).transpose(1, 0, 2)
    keep = lax.dynamic_slice_in_dim(normed, 2 * core, 2, axis=0)
    give = lax.dynamic_slice_in_dim(normed, 2 - 2 * core, 2, axis=0)
    give = after(give, other_qkv, other_out)
    parts = [keep, swap(give, 1), swap(keep, 2), swap(give, 3)]

    cut = width // 16
    piece_t = jnp.where(
        place < 12,
        lax.dynamic_slice(qkv, (1, place * cut, 0), (1, cut, width))[0],
        lax.dynamic_slice(out_weight, (1, (place - 12) * cut, 0), (1, cut, width))[0],
    )
    far_t = gather(after(swap(piece_t, 2), *parts))
    cut = width // 8
    piece_f = jnp.where(
        place < 8,
        lax.dynamic_slice_in_dim(mlp_in_weight, place * cut, cut, axis=0),
        lax.dynamic_slice_in_dim(mlp_out_weight, (place - 8) * cut, cut, axis=0),
    )
    moved = swap(piece_f, 2)
    back = attend(0, parts, near)
    far_f = gather(after(moved, back[0]))
    back = [(back[0] if d == 0 else swap(back[d], d)) for d in range(4)]
    back = [part.astype(F32) for part in back]
    mine = back[0] + back[2]
    theirs = back[1] + back[3]
    first = jnp.where(core == 0, mine, theirs)
    second = jnp.where(core == 0, theirs, mine)
    projected = jnp.concatenate([first, second], axis=0).transpose(1, 0, 2)
    middle = latents + modulation[0, 2] * projected + time_embed[None]
    normed = modulate(middle, modulation[1])
    other_mlp_in = swap(mlp_in_weight, 1)
    other_mlp_out = swap(mlp_out_weight, 1)
    regrouped = lax.all_to_all(normed, "seq", split_axis=0, concat_axis=0, tiled=True)
    regrouped = after(regrouped.reshape(1, -1, width), other_mlp_in, other_mlp_out)
    partial = attend(1, [regrouped], near, kind=F32)
    far_t = after(far_t, regrouped)
    far_other_t = swap(far_t, 1)
    (projected,) = attend(1, [regrouped], (far_t, far_other_t), inits=partial)
    projected = projected.reshape(normed.shape)
    projected = lax.all_to_all(projected, "seq", split_axis=0, concat_axis=0, tiled=True)
    far_f = after(far_f, projected)
    far_other_f = swap(far_f, 1)
    after_t = middle + modulation[1, 2] * projected.astype(F32)
    normed = modulate(after_t, modulation[2]).reshape(-1, width)
    weights = (mlp_in_weight, mlp_out_weight, other_mlp_in, other_mlp_out, far_f)
    partial = mlp(normed, weights)
    projected = mlp(normed, (far_other_f,), (partial,)).reshape(after_t.shape)
    return after_t + modulation[2, 2] * projected


def solution(mesh):
    in_specs = (
        P("tp", "seq", None),
        P("seq", None),
        P(),
        P(None, None, None, "tp"),
        P(None, "tp", None),
        P(None, "tp"),
        P("tp", None),
    )
    out_specs = P("tp", "seq", None)
    return jax.shard_map(
        on_device, mesh=mesh, in_specs=in_specs, out_specs=out_specs, check_vma=False
    )
```

```python
import functools
import math

import jax
import jax.numpy as jnp
from jax import lax
from jax.experimental import pallas as pl
from jax.experimental.pallas import tpu as pltpu
from jax.sharding import PartitionSpec as P

HD = 72
BF = jnp.bfloat16
F32 = jnp.float32
PLANE = [[x * 16 + z * 4 + y for x in range(4) for y in range(4)] for z in range(4)]
SWAPS = {d: [(t, t ^ d) for t in range(4)] for d in (1, 2, 3)}


def dot(a, b, ca, cb):
    return lax.dot_general(a, b, (((ca,), (cb,)), ((), ())), preferred_element_type=F32)


def attend_kernel(pieces, ready, layer, *refs):
    x_refs, refs = refs[:pieces], refs[pieces:]
    inits, refs = refs[:ready], refs[ready:]
    out_refs, (held, sems, stage, out_sems, came) = refs[-pieces - 5 : -5], refs[-5:]
    sources = refs[: -pieces - 5]
    heads = 4
    width = heads * HD
    length = 256
    plan = []
    if len(sources) == 4:
        for k in range(2):
            plan.append((sources[2 * k].at[layer], held.at[k, pl.ds(0, 3 * width)]))
            plan.append((sources[2 * k + 1].at[layer], held.at[k, pl.ds(3 * width, width)]))
    else:
        for k in range(2):
            plan.append((sources[k], held.at[k]))
    wide = pieces == 1
    items = 1 if wide else 2
    arrivals = []
    if not wide:
        part = stage.shape[1] // items
        for d, ref in enumerate(x_refs):
            rows = ref.at[pl.ds(0, items * part)]
            arrivals.append(pltpu.make_async_copy(rows, came.at[d], out_sems.at[d]))
            arrivals[-1].start()
    copies = [pltpu.make_async_copy(a, b, sems.at[i]) for i, (a, b) in enumerate(plan)]
    each = len(copies) // 2
    for copy in copies[:each]:
        copy.start()
    model = held.shape[2]
    if wide:
        part = x_refs[0].shape[0]
        spans = [slice(j * model, (j + 1) * model) for j in range(length // part)]
        x = jnp.concatenate([x_refs[0][:, span] for span in spans], axis=0)
    else:
        for arrival in arrivals:
            arrival.wait()
        spans = [slice(s * part, (s + 1) * part) for s in range(items)]
        x = jnp.concatenate([came[d, span] for span in spans for d in range(pieces)], axis=0)

    def shard(k):
        for copy in copies[each * k : each * (k + 1)]:
            copy.wait()
        for copy in copies[each * (k + 1) : each * (k + 2)]:
            copy.start()
        packed = dot(held[k, : 3 * width, :], x, 1, 1)
        columns = []
        for s in range(items):
            item = packed[:, s * length : (s + 1) * length]
            mixed = []
            for h in range(heads):
                q = item[h * HD : (h + 1) * HD] * (math.log2(math.e) / math.sqrt(HD))
                kk = item[width + h * HD : width + (h + 1) * HD]
                v = item[2 * width + h * HD : 2 * width + (h + 1) * HD].astype(BF)
                qh = q.astype(BF).astype(F32)
                kh = kk.astype(BF).astype(F32)
                left = jnp.concatenate([kh, kh, kk - kh], axis=0).astype(BF)
                right = jnp.concatenate([qh, q - qh, qh], axis=0).astype(BF)
                scores = dot(left, right, 0, 0)
                top = jnp.max(scores, axis=0, keepdims=True)
                weights = jnp.exp2(scores - top)
                total = jnp.sum(weights, axis=0, keepdims=True)
                mixed.append(dot(v, weights.astype(BF), 1, 0) / total)
            columns.append(jnp.concatenate(mixed, axis=0).astype(BF))
        return dot(jnp.concatenate(columns, axis=1), held[k, 3 * width :, :], 0, 0)

    total = shard(0) + shard(1)
    if ready:
        total = total + inits[0][...]
    total = total.astype(out_refs[0].dtype)
    if not wide:
        sends = []
        for d in reversed(range(pieces)):
            for s in range(items):
                start = s * length + d * part
                stage[d, s * part : (s + 1) * part] = total[start : start + part]
            sends.append(pltpu.make_async_copy(stage.at[d], out_refs[d], out_sems.at[d]))
            sends[-1].start()
        for send in sends:
            send.wait()
    elif ready:
        for j, span in enumerate(spans):
            out_refs[0][:, span] = total[j * part : (j + 1) * part]
    else:
        out_refs[0][...] = total


def attend(layer, parts, weights, inits=()):
    width = weights[0].shape[-1]
    pieces = len(parts)
    vmem = pl.BlockSpec(memory_space=pltpu.VMEM)
    free = pl.BlockSpec(memory_space=pl.ANY)
    hbm = pl.BlockSpec(memory_space=pltpu.HBM)
    rows = parts[0].size * pieces // width
    limit = 62 if pieces > 1 else 24 if inits else 48
    outs = [jax.ShapeDtypeStruct(parts[0].shape, BF)] * pieces
    if pieces == 1 and not inits:
        outs = [jax.ShapeDtypeStruct((rows, width), F32)]
    return pl.pallas_call(
        functools.partial(attend_kernel, pieces, len(inits), layer),
        out_shape=outs,
        in_specs=[vmem if pieces == 1 else free] * pieces
        + [vmem] * len(inits)
        + [free] * len(weights),
        out_specs=[vmem if pieces == 1 else hbm] * pieces,
        scratch_shapes=[
            pltpu.VMEM((2, width, width), BF),
            pltpu.SemaphoreType.DMA((len(weights),)),
            pltpu.VMEM((pieces, *parts[0].shape) if pieces > 1 else (1, 16, 128), BF),
            pltpu.SemaphoreType.DMA((pieces,)),
            pltpu.VMEM((pieces, *parts[0].shape) if pieces > 1 else (1, 16, 128), BF),
        ],
        compiler_params=pltpu.CompilerParams(vmem_limit_bytes=limit * 2**20),
        cost_estimate=pl.CostEstimate(
            flops=6 * rows * width * width,
            bytes_accessed=4 * width * width,
            transcendentals=0,
        ),
    )(*parts, *inits, *weights)


def norm_rows(x, mod_ref, b):
    average = jnp.mean(x, axis=-1, keepdims=True)
    centred = x - average
    spread = jnp.mean(centred * centred, axis=-1, keepdims=True)
    scaled = centred * lax.rsqrt(spread + 1e-06)
    return (scaled * (1.0 + mod_ref[b, 1:2, :]) + mod_ref[b, 0:1, :]).astype(BF)


def enter_kernel(core_ref, lat_ref, mod_ref, piece_ref, keep_ref, give_ref, send_ref):
    low = core_ref[0] == 0
    part = lat_ref.shape[0]
    rows = [norm_rows(lat_ref[:, f, :], mod_ref, 0) for f in range(4)]
    for i in range(2):
        span = slice(i * part, (i + 1) * part)
        keep = jnp.where(low, rows[i], rows[2 + i])
        keep_ref[span] = keep
        send_ref[span] = keep
        give_ref[span] = jnp.where(low, rows[2 + i], rows[i])
    send_ref[2 * part :] = piece_ref[...]


def enter_spatial(core, latents, modulation, piece):
    local, _, width = latents.shape
    vmem = pl.BlockSpec(memory_space=pltpu.VMEM)
    half = jax.ShapeDtypeStruct((2 * local, width), BF)
    return pl.pallas_call(
        enter_kernel,
        out_shape=[half, half, jax.ShapeDtypeStruct((2 * local + piece.shape[0], width), BF)],
        in_specs=[pl.BlockSpec(memory_space=pltpu.SMEM)] + [vmem] * 3,
        out_specs=[vmem] * 3,
        compiler_params=pltpu.CompilerParams(vmem_limit_bytes=62 * 2**20),
    )(core.reshape(1), latents, modulation, piece)


def middle_kernel(core_ref, embed_ref, mod_ref, *refs):
    sources, (mid_ref, norm_ref), held, sems = refs[:5], refs[5:7], refs[7:12], refs[12]
    copies = [
        pltpu.make_async_copy(a, b, sems.at[i]) for i, (a, b) in enumerate(zip(sources, held))
    ]
    for copy in copies:
        copy.start()
    for copy in copies:
        copy.wait()
    lat_ref, b0, b1, b2, b3 = held
    part, _, model = lat_ref.shape
    low = core_ref[0] == 0
    for f in range(4):
        span = slice((f % 2) * part, (f % 2 + 1) * part)
        mine = b0[span].astype(F32) + b2[span].astype(F32)
        theirs = b1[span].astype(F32) + b3[span].astype(F32)
        added = jnp.where(low, mine, theirs) if f < 2 else jnp.where(low, theirs, mine)
        x = lat_ref[:, f, :] + mod_ref[0, 2:3, :] * added + embed_ref[f : f + 1, :]
        mid_ref[f] = x
        norm_ref[:, f * model : (f + 1) * model] = norm_rows(x, mod_ref, 1)


def finish_spatial(core, latents, time_embed, modulation, back):
    local, frames, width = latents.shape
    vmem = pl.BlockSpec(memory_space=pltpu.VMEM)
    return pl.pallas_call(
        middle_kernel,
        out_shape=[
            jax.ShapeDtypeStruct((frames, local, width), F32),
            jax.ShapeDtypeStruct((local, frames * width), BF),
        ],
        in_specs=[pl.BlockSpec(memory_space=pltpu.SMEM)]
        + [vmem] * 2
        + [pl.BlockSpec(memory_space=pl.ANY)] * 5,
        out_specs=[vmem] * 2,
        scratch_shapes=[pltpu.VMEM(latents.shape, F32)]
        + [pltpu.VMEM(part.shape, BF) for part in back]
        + [pltpu.SemaphoreType.DMA((5,))],
        compiler_params=pltpu.CompilerParams(vmem_limit_bytes=62 * 2**20),
    )(core.reshape(1), time_embed, modulation, latents, *back)


def mlp_kernel(first, count, mod_ref, in_a, in_b, *refs):
    sources, refs = refs[:count], refs[count:]
    outs, (held, sems, held_a, held_b, in_sems) = refs[:-5], refs[-5:]
    width = held.shape[2]
    blocks = []
    for ref in sources:
        for part in range(ref.shape[0] // width):
            blocks.append(ref.at[pl.ds(part * width, width)])
    arrivals = [
        pltpu.make_async_copy(in_a, held_a, in_sems.at[0]),
        pltpu.make_async_copy(in_b, held_b, in_sems.at[1]),
    ]
    copies = [pltpu.make_async_copy(b, held.at[i], sems.at[i]) for i, b in enumerate(blocks)]
    for copy in arrivals + copies[:2]:
        copy.start()
    arrivals[0].wait()
    if first:
        arrivals[1].wait()
        base_ref, x_ref = outs
        local = held_b.shape[0]
        for f in range(held_a.shape[0]):
            arrived = held_b[:, f * width : (f + 1) * width].astype(F32)
            hidden = held_a[f] + mod_ref[1, 2:3, :] * arrived
            base_ref[f * local : (f + 1) * local] = hidden
            x_ref[f * local : (f + 1) * local] = norm_rows(hidden, mod_ref, 2)
    else:
        x_ref, base_ref = held_a, held_b
    x = x_ref[...]
    total = None
    for k in range(0, len(blocks), 2):
        copies[k].wait()
        if k + 2 < len(blocks):
            copies[k + 2].start()
        v = dot(x, held[k], 1, 0)
        inner = 0.5 * v * (1.0 + jnp.tanh(math.sqrt(2.0 / math.pi) * (v + 0.044715 * (v * v * v))))
        copies[k + 1].wait()
        if k + 3 < len(blocks):
            copies[k + 3].start()
        part = dot(inner.astype(BF), held[k + 1], 1, 0)
        total = part if total is None else total + part
    if first:
        base_ref[...] = base_ref[...] + mod_ref[2, 2:3, :] * total
    else:
        arrivals[1].wait()
        total = base_ref[...] + mod_ref[2, 2:3, :] * total
        out_ref = outs[0]
        local, frames = out_ref.shape[:2]
        for f in range(frames):
            out_ref[:, f, :] = total[f * local : (f + 1) * local]


def mlp(first, modulation, inputs, early, late, outs):
    weights = (*early, *late)
    width = weights[0].shape[1]
    blocks = sum(w.shape[0] for w in weights) // width
    vmem = pl.BlockSpec(memory_space=pltpu.VMEM)
    limit = 48 if first else 24
    return pl.pallas_call(
        functools.partial(mlp_kernel, first, len(weights)),
        out_shape=outs,
        in_specs=[vmem] + [pl.BlockSpec(memory_space=pl.ANY)] * (2 + len(weights)),
        out_specs=[vmem] * len(outs),
        scratch_shapes=[
            pltpu.VMEM((blocks, width, width), BF),
            pltpu.SemaphoreType.DMA((blocks,)),
            pltpu.VMEM(inputs[0].shape, inputs[0].dtype),
            pltpu.VMEM(inputs[1].shape, inputs[1].dtype),
            pltpu.SemaphoreType.DMA((2,)),
        ],
        compiler_params=pltpu.CompilerParams(vmem_limit_bytes=limit * 2**20),
        cost_estimate=pl.CostEstimate(
            flops=512 * width * width * blocks,
            bytes_accessed=2 * blocks * width * width,
            transcendentals=0,
        ),
    )(modulation, *inputs, *weights)


def swap(x, d):
    return lax.ppermute(x, "tp", SWAPS[d])


def gather(piece):
    return lax.all_gather(piece, "seq", axis=0, tiled=True, axis_index_groups=PLANE)


def no_work(*refs):
    del refs


def after(x, *others):
    return pl.pallas_call(
        no_work,
        out_shape=jax.ShapeDtypeStruct(x.shape, x.dtype),
        in_specs=[pl.BlockSpec(memory_space=pl.ANY)] * (1 + len(others)),
        out_specs=pl.BlockSpec(memory_space=pl.ANY),
        input_output_aliases={0: 0},
    )(x, *others)


def on_device(
    latents, time_embed, modulation, qkv_weight, out_weight, mlp_in_weight, mlp_out_weight
):
    width = latents.shape[2]
    seq = lax.axis_index("seq")
    tp = lax.axis_index("tp")
    place = (seq // 16) * 4 + seq % 4
    core = tp % 2

    qkv = qkv_weight.transpose(0, 2, 3, 1).reshape(2, -1, width)
    other_qkv = swap(qkv, 1)
    other_out = swap(out_weight, 1)
    near = (qkv, out_weight, other_qkv, other_out)

    cut = width // 16
    piece_t = jnp.where(
        place < 12,
        lax.dynamic_slice(qkv, (1, place * cut, 0), (1, cut, width))[0],
        lax.dynamic_slice(out_weight, (1, (place - 12) * cut, 0), (1, cut, width))[0],
    )
    keep, give, send = enter_spatial(core, latents, modulation, piece_t)
    give = after(give, other_qkv, other_out)
    parts = [keep, swap(give, 1), swap(send, 2), swap(give, 3)]
    far_t = gather(after(parts[2][2 * latents.shape[0] :], parts[1], parts[3]))

    cut = width // 8
    piece_f = jnp.where(
        place < 8,
        lax.dynamic_slice_in_dim(mlp_in_weight, place * cut, cut, axis=0),
        lax.dynamic_slice_in_dim(mlp_out_weight, (place - 8) * cut, cut, axis=0),
    )
    moved = swap(piece_f, 2)
    back = attend(0, parts, near)
    back = [(back[0] if d == 0 else swap(back[d], d)) for d in range(4)]
    far_f = gather(after(moved, *back[1:]))
    middle, normed = finish_spatial(core, latents, time_embed, modulation, back)
    other_mlp_in = swap(mlp_in_weight, 1)
    other_mlp_out = swap(mlp_out_weight, 1)

    def regroup(rows):
        rows = rows.reshape(latents.shape)
        rows = lax.all_to_all(rows, "seq", split_axis=0, concat_axis=0, tiled=True)
        return rows.reshape(rows.shape[0], -1)

    regrouped = after(regroup(normed), other_mlp_in, other_mlp_out)
    partial = attend(1, [regrouped], near)
    far_t = after(far_t, regrouped)
    far_other_t = swap(far_t, 1)
    (projected,) = attend(1, [regrouped], (far_t, far_other_t), partial)
    projected = regroup(projected)
    far_f = after(far_f, projected)
    far_other_f = swap(far_f, 1)
    rows = latents.shape[0] * latents.shape[1]
    base = jax.ShapeDtypeStruct((rows, width), F32)
    x = jax.ShapeDtypeStruct((rows, width), BF)
    early = (mlp_in_weight, mlp_out_weight, other_mlp_in, other_mlp_out)
    base, x = mlp(True, modulation, (middle, projected), early, (far_f,), [base, x])
    result = jax.ShapeDtypeStruct(latents.shape, F32)
    return mlp(False, modulation, (x, base), (), (far_other_f,), [result])[0]


def solution(mesh):
    in_specs = (
        P("tp", "seq", None),
        P("seq", None),
        P(),
        P(None, None, None, "tp"),
        P(None, "tp", None),
        P(None, "tp"),
        P("tp", None),
    )
    out_specs = P("tp", "seq", None)
    return jax.shard_map(
        on_device, mesh=mesh, in_specs=in_specs, out_specs=out_specs, check_vma=False
    )
```

```python
import functools
import math

import jax
import jax.numpy as jnp
from jax import lax
from jax.experimental import pallas as pl
from jax.experimental.pallas import tpu as pltpu
from jax.sharding import PartitionSpec as P

HD = 72
BF = jnp.bfloat16
F32 = jnp.float32
PLANE = [[x * 16 + z * 4 + y for x in range(4) for y in range(4)] for z in range(4)]
SWAPS = {d: [(t, t ^ d) for t in range(4)] for d in (1, 2, 3)}


def dot(a, b, ca, cb):
    return lax.dot_general(a, b, (((ca,), (cb,)), ((), ())), preferred_element_type=F32)


def attend_kernel(pieces, ready, layer, *refs):
    x_refs, refs = refs[:pieces], refs[pieces:]
    inits, refs = refs[:ready], refs[ready:]
    results = 2 if pieces == 1 and not ready else pieces
    out_refs, (held, sems, stage, out_sems, came, rows4) = refs[-results - 6 : -6], refs[-6:]
    sources = refs[: -results - 6]
    heads = 4
    width = heads * HD
    length = 256
    plan = []
    if len(sources) == 4:
        for k in range(2):
            plan.append((sources[2 * k].at[layer], held.at[k, pl.ds(0, 3 * width)]))
            plan.append((sources[2 * k + 1].at[layer], held.at[k, pl.ds(3 * width, width)]))
    else:
        for k in range(2):
            plan.append((sources[k], held.at[k]))
    wide = pieces == 1
    items = 1 if wide else 2
    arrivals = []
    if not wide:
        part = stage.shape[1] // items
        for d, ref in enumerate(x_refs):
            rows = ref.at[pl.ds(0, items * part)]
            arrivals.append(pltpu.make_async_copy(rows, came.at[d], out_sems.at[d]))
            arrivals[-1].start()
    copies = [pltpu.make_async_copy(a, b, sems.at[i]) for i, (a, b) in enumerate(plan)]
    each = len(copies) // 2
    for copy in copies[:each]:
        copy.start()
    model = held.shape[2]
    if ready:
        x = x_refs[0][...]
    elif wide:
        frames = x_refs[0].shape[1]
        rows4[...] = x_refs[0][...].astype(F32)
        x = jnp.concatenate([rows4[:, j, :].astype(BF) for j in range(frames)], axis=0)
        out_refs[1][...] = x
    else:
        for arrival in arrivals:
            arrival.wait()
        spans = [slice(s * part, (s + 1) * part) for s in range(items)]
        x = jnp.concatenate([came[d, span] for span in spans for d in range(pieces)], axis=0)

    def shard(k):
        for copy in copies[each * k : each * (k + 1)]:
            copy.wait()
        for copy in copies[each * (k + 1) : each * (k + 2)]:
            copy.start()
        packed = dot(held[k, : 3 * width, :], x, 1, 1)
        columns = []
        for s in range(items):
            item = packed[:, s * length : (s + 1) * length]
            mixed = []
            for h in range(heads):
                q = item[h * HD : (h + 1) * HD] * (math.log2(math.e) / math.sqrt(HD))
                kk = item[width + h * HD : width + (h + 1) * HD]
                v = item[2 * width + h * HD : 2 * width + (h + 1) * HD].astype(BF)
                qh = q.astype(BF).astype(F32)
                kh = kk.astype(BF).astype(F32)
                left = jnp.concatenate([kh, kh, kk - kh], axis=0).astype(BF)
                right = jnp.concatenate([qh, q - qh, qh], axis=0).astype(BF)
                scores = dot(left, right, 0, 0)
                top = jnp.max(scores, axis=0, keepdims=True)
                weights = jnp.exp2(scores - top)
                total = jnp.sum(weights, axis=0, keepdims=True)
                mixed.append(dot(v, weights.astype(BF), 1, 0) / total)
            columns.append(jnp.concatenate(mixed, axis=0).astype(BF))
        return dot(jnp.concatenate(columns, axis=1), held[k, 3 * width :, :], 0, 0)

    total = shard(0) + shard(1)
    if ready:
        total = total + inits[0][...]
    if not wide:
        total = total.astype(BF)
        sends = []
        for d in reversed(range(pieces)):
            for s in range(items):
                start = s * length + d * part
                stage[d, s * part : (s + 1) * part] = total[start : start + part]
            sends.append(pltpu.make_async_copy(stage.at[d], out_refs[d], out_sems.at[d]))
            sends[-1].start()
        for send in sends:
            send.wait()
    elif ready:
        total = total.astype(BF)
        part = out_refs[0].shape[0]
        for j in range(length // part):
            out_refs[0][:, j * model : (j + 1) * model] = total[j * part : (j + 1) * part]
    else:
        out_refs[0][...] = total


def attend(layer, parts, weights, inits=()):
    width = weights[0].shape[-1]
    pieces = len(parts)
    vmem = pl.BlockSpec(memory_space=pltpu.VMEM)
    free = pl.BlockSpec(memory_space=pl.ANY)
    hbm = pl.BlockSpec(memory_space=pltpu.HBM)
    rows = parts[0].size * pieces // width
    limit = 62 if pieces > 1 else 24 if inits else 48
    outs = [jax.ShapeDtypeStruct(parts[0].shape, BF)] * pieces
    if pieces == 1:
        outs = [jax.ShapeDtypeStruct((rows, width), kind) for kind in (F32, BF)]
    if inits:
        outs = [jax.ShapeDtypeStruct((rows // 4, 4 * width), BF)]
    return pl.pallas_call(
        functools.partial(attend_kernel, pieces, len(inits), layer),
        out_shape=outs,
        in_specs=[vmem if pieces == 1 else free] * pieces
        + [vmem] * len(inits)
        + [free] * len(weights),
        out_specs=[vmem if pieces == 1 else hbm] * len(outs),
        scratch_shapes=[
            pltpu.VMEM((2, width, width), BF),
            pltpu.SemaphoreType.DMA((len(weights),)),
            pltpu.VMEM((pieces, *parts[0].shape) if pieces > 1 else (1, 16, 128), BF),
            pltpu.SemaphoreType.DMA((pieces,)),
            pltpu.VMEM((pieces, *parts[0].shape) if pieces > 1 else (1, 16, 128), BF),
            pltpu.VMEM(parts[0].shape if len(outs) == 2 else (8, 4, 128), F32),
        ],
        compiler_params=pltpu.CompilerParams(vmem_limit_bytes=limit * 2**20),
        cost_estimate=pl.CostEstimate(
            flops=6 * rows * width * width,
            bytes_accessed=4 * width * width,
            transcendentals=0,
        ),
    )(*parts, *inits, *weights)


def norm_rows(x, mod_ref, b):
    average = jnp.mean(x, axis=-1, keepdims=True)
    centred = x - average
    spread = jnp.mean(centred * centred, axis=-1, keepdims=True)
    scaled = centred * lax.rsqrt(spread + 1e-06)
    return (scaled * (1.0 + mod_ref[b, 1:2, :]) + mod_ref[b, 0:1, :]).astype(BF)


def enter_kernel(core_ref, lat_ref, mod_ref, piece_ref, keep_ref, give_ref, send_ref):
    low = core_ref[0] == 0
    part = lat_ref.shape[0]
    rows = [norm_rows(lat_ref[:, f, :], mod_ref, 0) for f in range(4)]
    for i in range(2):
        span = slice(i * part, (i + 1) * part)
        keep = jnp.where(low, rows[i], rows[2 + i])
        keep_ref[span] = keep
        send_ref[span] = keep
        give_ref[span] = jnp.where(low, rows[2 + i], rows[i])
    send_ref[2 * part :] = piece_ref[...]


def enter_spatial(core, latents, modulation, piece):
    local, _, width = latents.shape
    vmem = pl.BlockSpec(memory_space=pltpu.VMEM)
    half = jax.ShapeDtypeStruct((2 * local, width), BF)
    return pl.pallas_call(
        enter_kernel,
        out_shape=[half, half, jax.ShapeDtypeStruct((2 * local + piece.shape[0], width), BF)],
        in_specs=[pl.BlockSpec(memory_space=pltpu.SMEM)] + [vmem] * 3,
        out_specs=[vmem] * 3,
        compiler_params=pltpu.CompilerParams(vmem_limit_bytes=62 * 2**20),
    )(core.reshape(1), latents, modulation, piece)


def middle_kernel(core_ref, embed_ref, mod_ref, *refs):
    sources, (mid_ref, norm_ref), held, sems, wide = refs[:5], refs[5:7], refs[7:12], refs[12], refs[13]
    copies = [
        pltpu.make_async_copy(a, b, sems.at[i]) for i, (a, b) in enumerate(zip(sources, held))
    ]
    for copy in copies:
        copy.start()
    for copy in copies:
        copy.wait()
    lat_ref, b0, b1, b2, b3 = held
    part = lat_ref.shape[0]
    low = core_ref[0] == 0
    for f in range(4):
        span = slice((f % 2) * part, (f % 2 + 1) * part)
        mine = b0[span].astype(F32) + b2[span].astype(F32)
        theirs = b1[span].astype(F32) + b3[span].astype(F32)
        added = jnp.where(low, mine, theirs) if f < 2 else jnp.where(low, theirs, mine)
        x = lat_ref[:, f, :] + mod_ref[0, 2:3, :] * added + embed_ref[f : f + 1, :]
        mid_ref[f] = x
        wide[:, f, :] = norm_rows(x, mod_ref, 1).astype(F32)
    norm_ref[...] = wide[...].astype(BF)


def finish_spatial(core, latents, time_embed, modulation, back):
    local, frames, width = latents.shape
    vmem = pl.BlockSpec(memory_space=pltpu.VMEM)
    return pl.pallas_call(
        middle_kernel,
        out_shape=[
            jax.ShapeDtypeStruct((frames, local, width), F32),
            jax.ShapeDtypeStruct((local, frames, width), BF),
        ],
        in_specs=[pl.BlockSpec(memory_space=pltpu.SMEM)]
        + [vmem] * 2
        + [pl.BlockSpec(memory_space=pl.ANY)] * 5,
        out_specs=[vmem] * 2,
        scratch_shapes=[pltpu.VMEM(latents.shape, F32)]
        + [pltpu.VMEM(part.shape, BF) for part in back]
        + [pltpu.SemaphoreType.DMA((5,)), pltpu.VMEM(latents.shape, F32)],
        compiler_params=pltpu.CompilerParams(vmem_limit_bytes=62 * 2**20),
    )(core.reshape(1), time_embed, modulation, latents, *back)


def mlp_kernel(first, count, mod_ref, in_a, in_b, *refs):
    sources, refs = refs[:count], refs[count:]
    outs, (held, sems, held_a, held_b, in_sems, rows4) = refs[:-6], refs[-6:]
    width = held.shape[2]
    blocks = []
    for ref in sources:
        for part in range(ref.shape[0] // width):
            blocks.append(ref.at[pl.ds(part * width, width)])
    arrivals = [
        pltpu.make_async_copy(in_a, held_a, in_sems.at[0]),
        pltpu.make_async_copy(in_b, held_b, in_sems.at[1]),
    ]
    copies = [pltpu.make_async_copy(b, held.at[i], sems.at[i]) for i, b in enumerate(blocks)]
    for copy in arrivals + copies[:2]:
        copy.start()
    arrivals[0].wait()
    if first:
        arrivals[1].wait()
        base_ref, x_ref = outs
        local = held_b.shape[0]
        rows4[...] = held_b[...].astype(F32)
        for f in range(held_a.shape[0]):
            hidden = held_a[f] + mod_ref[1, 2:3, :] * rows4[:, f, :]
            base_ref[f * local : (f + 1) * local] = hidden
            x_ref[f * local : (f + 1) * local] = norm_rows(hidden, mod_ref, 2)
    else:
        x_ref, base_ref = held_a, held_b
    x = x_ref[...]
    total = None
    for k in range(0, len(blocks), 2):
        copies[k].wait()
        if k + 2 < len(blocks):
            copies[k + 2].start()
        v = dot(x, held[k], 1, 0)
        inner = 0.5 * v * (1.0 + jnp.tanh(math.sqrt(2.0 / math.pi) * (v + 0.044715 * (v * v * v))))
        copies[k + 1].wait()
        if k + 3 < len(blocks):
            copies[k + 3].start()
        part = dot(inner.astype(BF), held[k + 1], 1, 0)
        total = part if total is None else total + part
    if first:
        base_ref[...] = base_ref[...] + mod_ref[2, 2:3, :] * total
    else:
        arrivals[1].wait()
        total = base_ref[...] + mod_ref[2, 2:3, :] * total
        out_ref = outs[0]
        local, frames = out_ref.shape[:2]
        for f in range(frames):
            out_ref[:, f, :] = total[f * local : (f + 1) * local]


def mlp(first, modulation, inputs, early, late, outs):
    weights = (*early, *late)
    width = weights[0].shape[1]
    blocks = sum(w.shape[0] for w in weights) // width
    vmem = pl.BlockSpec(memory_space=pltpu.VMEM)
    limit = 48 if first else 24
    return pl.pallas_call(
        functools.partial(mlp_kernel, first, len(weights)),
        out_shape=outs,
        in_specs=[vmem] + [pl.BlockSpec(memory_space=pl.ANY)] * (2 + len(weights)),
        out_specs=[vmem] * len(outs),
        scratch_shapes=[
            pltpu.VMEM((blocks, width, width), BF),
            pltpu.SemaphoreType.DMA((blocks,)),
            pltpu.VMEM(inputs[0].shape, inputs[0].dtype),
            pltpu.VMEM(inputs[1].shape, inputs[1].dtype),
            pltpu.SemaphoreType.DMA((2,)),
            pltpu.VMEM(inputs[1].shape if first else (8, 4, 128), F32),
        ],
        compiler_params=pltpu.CompilerParams(vmem_limit_bytes=limit * 2**20),
        cost_estimate=pl.CostEstimate(
            flops=512 * width * width * blocks,
            bytes_accessed=2 * blocks * width * width,
            transcendentals=0,
        ),
    )(modulation, *inputs, *weights)


def swap(x, d):
    return lax.ppermute(x, "tp", SWAPS[d])


def gather(piece):
    return lax.all_gather(piece, "seq", axis=0, tiled=True, axis_index_groups=PLANE)


def no_work(*refs):
    del refs


def after(x, *others):
    return pl.pallas_call(
        no_work,
        out_shape=jax.ShapeDtypeStruct(x.shape, x.dtype),
        in_specs=[pl.BlockSpec(memory_space=pl.ANY)] * (1 + len(others)),
        out_specs=pl.BlockSpec(memory_space=pl.ANY),
        input_output_aliases={0: 0},
    )(x, *others)


def on_device(
    latents, time_embed, modulation, qkv_weight, out_weight, mlp_in_weight, mlp_out_weight
):
    width = latents.shape[2]
    seq = lax.axis_index("seq")
    tp = lax.axis_index("tp")
    place = (seq // 16) * 4 + seq % 4
    core = tp % 2

    qkv = qkv_weight.transpose(0, 2, 3, 1).reshape(2, -1, width)
    other_qkv = swap(qkv, 1)
    other_out = swap(out_weight, 1)
    near = (qkv, out_weight, other_qkv, other_out)

    cut = width // 16
    piece_t = jnp.where(
        place < 12,
        lax.dynamic_slice(qkv, (1, place * cut, 0), (1, cut, width))[0],
        lax.dynamic_slice(out_weight, (1, (place - 12) * cut, 0), (1, cut, width))[0],
    )
    cut = width // 8
    piece_f = jnp.where(
        place < 8,
        lax.dynamic_slice_in_dim(mlp_in_weight, place * cut, cut, axis=0),
        lax.dynamic_slice_in_dim(mlp_out_weight, (place - 8) * cut, cut, axis=0),
    )
    keep, give, send = enter_spatial(core, latents, modulation, piece_t)
    give = after(give, other_qkv, other_out, piece_f)
    parts = [keep, swap(give, 1), swap(send, 2), swap(give, 3)]
    far_t = gather(after(parts[2][2 * latents.shape[0] :], parts[1], parts[3]))

    moved = swap(piece_f, 2)
    back = attend(0, parts, near)
    far_f = gather(after(moved, back[0]))
    back = [(back[0] if d == 0 else swap(back[d], d)) for d in range(4)]
    middle, normed = finish_spatial(core, latents, time_embed, modulation, back)
    other_mlp_in = swap(mlp_in_weight, 1)
    other_mlp_out = swap(mlp_out_weight, 1)

    def regroup(rows):
        rows = rows.reshape(latents.shape)
        return lax.all_to_all(rows, "seq", split_axis=0, concat_axis=0, tiled=True)

    regrouped = regroup(normed)
    partial, rows = attend(1, [regrouped], near)
    far_t = after(far_t, middle, other_mlp_in, other_mlp_out)
    far_other_t = swap(far_t, 1)
    (projected,) = attend(1, [rows], (far_t, far_other_t), [partial])
    projected = regroup(projected)
    far_f = after(far_f, projected)
    far_other_f = swap(far_f, 1)
    rows = latents.shape[0] * latents.shape[1]
    base = jax.ShapeDtypeStruct((rows, width), F32)
    x = jax.ShapeDtypeStruct((rows, width), BF)
    early = (mlp_in_weight, mlp_out_weight, other_mlp_in, other_mlp_out)
    base, x = mlp(True, modulation, (middle, projected), early, (far_f,), [base, x])
    result = jax.ShapeDtypeStruct(latents.shape, F32)
    return mlp(False, modulation, (x, base), (), (far_other_f,), [result])[0]


def solution(mesh):
    in_specs = (
        P("tp", "seq", None),
        P("seq", None),
        P(),
        P(None, None, None, "tp"),
        P(None, "tp", None),
        P(None, "tp"),
        P("tp", None),
    )
    out_specs = P("tp", "seq", None)
    return jax.shard_map(
        on_device, mesh=mesh, in_specs=in_specs, out_specs=out_specs, check_vma=False
    )
```

```python
import functools
import math

import jax
import jax.numpy as jnp
from jax import lax
from jax.experimental import pallas as pl
from jax.experimental.pallas import tpu as pltpu
from jax.sharding import PartitionSpec as P

HD = 72
BF = jnp.bfloat16
F32 = jnp.float32
PLANE = [[x * 16 + z * 4 + y for x in range(4) for y in range(4)] for z in range(4)]
SWAPS = {d: [(t, t ^ d) for t in range(4)] for d in (1, 2, 3)}


def dot(a, b, ca, cb):
    return lax.dot_general(a, b, (((ca,), (cb,)), ((), ())), preferred_element_type=F32)


def attend_kernel(pieces, ready, layer, *refs):
    x_refs, refs = refs[:pieces], refs[pieces:]
    inits, refs = refs[:ready], refs[ready:]
    results = 2 if pieces == 1 and not ready else pieces
    out_refs, (held, sems, stage, out_sems, came, rows4) = refs[-results - 6 : -6], refs[-6:]
    sources = refs[: -results - 6]
    heads = 4
    width = heads * HD
    length = 256
    plan = []
    if len(sources) == 4:
        for k in range(2):
            plan.append((sources[2 * k].at[layer], held.at[k, pl.ds(0, 3 * width)]))
            plan.append((sources[2 * k + 1].at[layer], held.at[k, pl.ds(3 * width, width)]))
    else:
        for k in range(2):
            plan.append((sources[k], held.at[k]))
    wide = pieces == 1
    items = 1 if wide else 2
    arrivals = []
    if not wide:
        part = stage.shape[1] // items
        for d, ref in enumerate(x_refs):
            rows = ref.at[pl.ds(0, items * part)]
            arrivals.append(pltpu.make_async_copy(rows, came.at[d], out_sems.at[d]))
            arrivals[-1].start()
    copies = [pltpu.make_async_copy(a, b, sems.at[i]) for i, (a, b) in enumerate(plan)]
    each = len(copies) // 2
    for copy in copies[:each]:
        copy.start()
    model = held.shape[2]
    if ready:
        x = x_refs[0][...]
    elif wide:
        frames = x_refs[0].shape[1]
        rows4[...] = x_refs[0][...].astype(F32)
        x = jnp.concatenate([rows4[:, j, :].astype(BF) for j in range(frames)], axis=0)
        out_refs[1][...] = x
    else:
        for arrival in arrivals:
            arrival.wait()
        spans = [slice(s * part, (s + 1) * part) for s in range(items)]
        x = jnp.concatenate([came[d, span] for span in spans for d in range(pieces)], axis=0)

    def shard(k):
        for copy in copies[each * k : each * (k + 1)]:
            copy.wait()
        for copy in copies[each * (k + 1) : each * (k + 2)]:
            copy.start()
        packed = dot(held[k, : 3 * width, :], x, 1, 1)
        columns = []
        for s in range(items):
            item = packed[:, s * length : (s + 1) * length]
            mixed = []
            for h in range(heads):
                q = item[h * HD : (h + 1) * HD] * (math.log2(math.e) / math.sqrt(HD))
                kk = item[width + h * HD : width + (h + 1) * HD]
                v = item[2 * width + h * HD : 2 * width + (h + 1) * HD].astype(BF)
                qh = q.astype(BF).astype(F32)
                kh = kk.astype(BF).astype(F32)
                left = jnp.concatenate([kh, kh, kk - kh], axis=0).astype(BF)
                right = jnp.concatenate([qh, q - qh, qh], axis=0).astype(BF)
                scores = dot(left, right, 0, 0)
                top = jnp.max(scores, axis=0, keepdims=True)
                weights = jnp.exp2(scores - top)
                total = jnp.sum(weights, axis=0, keepdims=True)
                mixed.append(dot(v, weights.astype(BF), 1, 0) / total)
            columns.append(jnp.concatenate(mixed, axis=0).astype(BF))
        return dot(jnp.concatenate(columns, axis=1), held[k, 3 * width :, :], 0, 0)

    total = shard(0) + shard(1)
    if ready:
        total = total + inits[0][...]
    if not wide:
        total = total.astype(BF)
        sends = []
        for d in reversed(range(pieces)):
            for s in range(items):
                start = s * length + d * part
                stage[d, s * part : (s + 1) * part] = total[start : start + part]
            sends.append(pltpu.make_async_copy(stage.at[d], out_refs[d], out_sems.at[d]))
            sends[-1].start()
        for send in sends:
            send.wait()
    elif ready:
        total = total.astype(BF)
        part = out_refs[0].shape[0]
        for j in range(length // part):
            out_refs[0][:, j * model : (j + 1) * model] = total[j * part : (j + 1) * part]
    else:
        out_refs[0][...] = total


def attend(layer, parts, weights, inits=()):
    width = weights[0].shape[-1]
    pieces = len(parts)
    vmem = pl.BlockSpec(memory_space=pltpu.VMEM)
    free = pl.BlockSpec(memory_space=pl.ANY)
    hbm = pl.BlockSpec(memory_space=pltpu.HBM)
    rows = parts[0].size * pieces // width
    limit = 62 if pieces > 1 else 24 if inits else 48
    outs = [jax.ShapeDtypeStruct(parts[0].shape, BF)] * pieces
    if pieces == 1:
        outs = [jax.ShapeDtypeStruct((rows, width), kind) for kind in (F32, BF)]
    if inits:
        outs = [jax.ShapeDtypeStruct((rows // 4, 4 * width), BF)]
    return pl.pallas_call(
        functools.partial(attend_kernel, pieces, len(inits), layer),
        out_shape=outs,
        in_specs=[vmem if pieces == 1 else free] * pieces
        + [vmem] * len(inits)
        + [free] * len(weights),
        out_specs=[vmem if pieces == 1 else hbm] * len(outs),
        scratch_shapes=[
            pltpu.VMEM((2, width, width), BF),
            pltpu.SemaphoreType.DMA((len(weights),)),
            pltpu.VMEM((pieces, *parts[0].shape) if pieces > 1 else (1, 16, 128), BF),
            pltpu.SemaphoreType.DMA((pieces,)),
            pltpu.VMEM((pieces, *parts[0].shape) if pieces > 1 else (1, 16, 128), BF),
            pltpu.VMEM(parts[0].shape if len(outs) == 2 else (8, 4, 128), F32),
        ],
        compiler_params=pltpu.CompilerParams(vmem_limit_bytes=limit * 2**20),
        cost_estimate=pl.CostEstimate(
            flops=6 * rows * width * width,
            bytes_accessed=4 * width * width,
            transcendentals=0,
        ),
    )(*parts, *inits, *weights)


def norm_rows(x, mod_ref, b):
    average = jnp.mean(x, axis=-1, keepdims=True)
    centred = x - average
    spread = jnp.mean(centred * centred, axis=-1, keepdims=True)
    scaled = centred * lax.rsqrt(spread + 1e-06)
    return (scaled * (1.0 + mod_ref[b, 1:2, :]) + mod_ref[b, 0:1, :]).astype(BF)


def enter_kernel(core_ref, lat_ref, mod_ref, piece_ref, keep_ref, give_ref, send_ref):
    low = core_ref[0] == 0
    part = lat_ref.shape[0]
    rows = [norm_rows(lat_ref[:, f, :], mod_ref, 0) for f in range(4)]
    for i in range(2):
        span = slice(i * part, (i + 1) * part)
        keep = jnp.where(low, rows[i], rows[2 + i])
        keep_ref[span] = keep
        send_ref[span] = keep
        give_ref[span] = jnp.where(low, rows[2 + i], rows[i])
    send_ref[2 * part :] = piece_ref[...]


def enter_spatial(core, latents, modulation, piece):
    local, _, width = latents.shape
    vmem = pl.BlockSpec(memory_space=pltpu.VMEM)
    half = jax.ShapeDtypeStruct((2 * local, width), BF)
    return pl.pallas_call(
        enter_kernel,
        out_shape=[half, half, jax.ShapeDtypeStruct((2 * local + piece.shape[0], width), BF)],
        in_specs=[pl.BlockSpec(memory_space=pltpu.SMEM)] + [vmem] * 3,
        out_specs=[vmem] * 3,
        compiler_params=pltpu.CompilerParams(vmem_limit_bytes=62 * 2**20),
    )(core.reshape(1), latents, modulation, piece)


def middle_kernel(core_ref, embed_ref, mod_ref, *refs):
    sources, (mid_ref, norm_ref), held, sems, wide = refs[:5], refs[5:7], refs[7:12], refs[12], refs[13]
    copies = [
        pltpu.make_async_copy(a, b, sems.at[i]) for i, (a, b) in enumerate(zip(sources, held))
    ]
    for copy in copies:
        copy.start()
    for copy in copies:
        copy.wait()
    lat_ref, b0, b1, b2, b3 = held
    part = lat_ref.shape[0]
    low = core_ref[0] == 0
    for f in range(4):
        span = slice((f % 2) * part, (f % 2 + 1) * part)
        mine = b0[span].astype(F32) + b2[span].astype(F32)
        theirs = b1[span].astype(F32) + b3[span].astype(F32)
        added = jnp.where(low, mine, theirs) if f < 2 else jnp.where(low, theirs, mine)
        x = lat_ref[:, f, :] + mod_ref[0, 2:3, :] * added + embed_ref[f : f + 1, :]
        mid_ref[f] = x
        wide[:, f, :] = norm_rows(x, mod_ref, 1).astype(F32)
    norm_ref[...] = wide[...].astype(BF)


def finish_spatial(core, latents, time_embed, modulation, back):
    local, frames, width = latents.shape
    vmem = pl.BlockSpec(memory_space=pltpu.VMEM)
    return pl.pallas_call(
        middle_kernel,
        out_shape=[
            jax.ShapeDtypeStruct((frames, local, width), F32),
            jax.ShapeDtypeStruct((local, frames, width), BF),
        ],
        in_specs=[pl.BlockSpec(memory_space=pltpu.SMEM)]
        + [vmem] * 2
        + [pl.BlockSpec(memory_space=pl.ANY)] * 5,
        out_specs=[vmem] * 2,
        scratch_shapes=[pltpu.VMEM(latents.shape, F32)]
        + [pltpu.VMEM(part.shape, BF) for part in back]
        + [pltpu.SemaphoreType.DMA((5,)), pltpu.VMEM(latents.shape, F32)],
        cost_estimate=pl.CostEstimate(
            flops=10**11, bytes_accessed=8 * latents.size, transcendentals=0
        ),
        compiler_params=pltpu.CompilerParams(vmem_limit_bytes=62 * 2**20),
    )(core.reshape(1), time_embed, modulation, latents, *back)


def mlp_kernel(first, count, mod_ref, in_a, in_b, *refs):
    sources, refs = refs[:count], refs[count:]
    outs, (held, sems, held_a, held_b, in_sems, rows4) = refs[:-6], refs[-6:]
    width = held.shape[2]
    blocks = []
    for ref in sources:
        for part in range(ref.shape[0] // width):
            blocks.append(ref.at[pl.ds(part * width, width)])
    arrivals = [
        pltpu.make_async_copy(in_a, held_a, in_sems.at[0]),
        pltpu.make_async_copy(in_b, held_b, in_sems.at[1]),
    ]
    copies = [pltpu.make_async_copy(b, held.at[i], sems.at[i]) for i, b in enumerate(blocks)]
    for copy in arrivals + copies[:3]:
        copy.start()
    arrivals[0].wait()
    if first:
        arrivals[1].wait()
        base_ref, x_ref = outs
        local = held_b.shape[0]
        rows4[...] = held_b[...].astype(F32)
        for f in range(held_a.shape[0]):
            hidden = held_a[f] + mod_ref[1, 2:3, :] * rows4[:, f, :]
            base_ref[f * local : (f + 1) * local] = hidden
            x_ref[f * local : (f + 1) * local] = norm_rows(hidden, mod_ref, 2)
    else:
        x_ref, base_ref = held_a, held_b
    x = x_ref[...]
    total = None
    for k in range(0, len(blocks), 2):
        copies[k].wait()
        if k + 3 < len(blocks):
            copies[k + 3].start()
        v = dot(x, held[k], 1, 0)
        inner = 0.5 * v * (1.0 + jnp.tanh(math.sqrt(2.0 / math.pi) * (v + 0.044715 * (v * v * v))))
        copies[k + 1].wait()
        if k + 4 < len(blocks):
            copies[k + 4].start()
        part = dot(inner.astype(BF), held[k + 1], 1, 0)
        total = part if total is None else total + part
    if first:
        base_ref[...] = base_ref[...] + mod_ref[2, 2:3, :] * total
    else:
        arrivals[1].wait()
        total = base_ref[...] + mod_ref[2, 2:3, :] * total
        out_ref = outs[0]
        local, frames = out_ref.shape[:2]
        for f in range(frames):
            out_ref[:, f, :] = total[f * local : (f + 1) * local]


def mlp(first, modulation, inputs, early, late, outs):
    weights = (*early, *late)
    width = weights[0].shape[1]
    blocks = sum(w.shape[0] for w in weights) // width
    vmem = pl.BlockSpec(memory_space=pltpu.VMEM)
    limit = 48 if first else 24
    return pl.pallas_call(
        functools.partial(mlp_kernel, first, len(weights)),
        out_shape=outs,
        in_specs=[vmem] + [pl.BlockSpec(memory_space=pl.ANY)] * (2 + len(weights)),
        out_specs=[vmem] * len(outs),
        scratch_shapes=[
            pltpu.VMEM((blocks, width, width), BF),
            pltpu.SemaphoreType.DMA((blocks,)),
            pltpu.VMEM(inputs[0].shape, inputs[0].dtype),
            pltpu.VMEM(inputs[1].shape, inputs[1].dtype),
            pltpu.SemaphoreType.DMA((2,)),
            pltpu.VMEM(inputs[1].shape if first else (8, 4, 128), F32),
        ],
        compiler_params=pltpu.CompilerParams(vmem_limit_bytes=limit * 2**20),
        cost_estimate=pl.CostEstimate(
            flops=512 * width * width * blocks,
            bytes_accessed=2 * blocks * width * width,
            transcendentals=0,
        ),
    )(modulation, *inputs, *weights)


def swap(x, d):
    return lax.ppermute(x, "tp", SWAPS[d])


def gather(piece):
    return lax.all_gather(piece, "seq", axis=0, tiled=True, axis_index_groups=PLANE)


def no_work(*refs):
    del refs


def after(x, *others):
    return pl.pallas_call(
        no_work,
        out_shape=jax.ShapeDtypeStruct(x.shape, x.dtype),
        in_specs=[pl.BlockSpec(memory_space=pl.ANY)] * (1 + len(others)),
        out_specs=pl.BlockSpec(memory_space=pl.ANY),
        input_output_aliases={0: 0},
    )(x, *others)


def on_device(
    latents, time_embed, modulation, qkv_weight, out_weight, mlp_in_weight, mlp_out_weight
):
    width = latents.shape[2]
    seq = lax.axis_index("seq")
    tp = lax.axis_index("tp")
    place = (seq // 16) * 4 + seq % 4
    core = tp % 2

    qkv = qkv_weight.transpose(0, 2, 3, 1).reshape(2, -1, width)
    other_qkv = swap(qkv, 1)
    other_out = swap(out_weight, 1)
    near = (qkv, out_weight, other_qkv, other_out)

    cut = width // 16
    piece_t = jnp.where(
        place < 12,
        lax.dynamic_slice(qkv, (1, place * cut, 0), (1, cut, width))[0],
        lax.dynamic_slice(out_weight, (1, (place - 12) * cut, 0), (1, cut, width))[0],
    )
    cut = width // 8
    piece_f = jnp.where(
        place < 8,
        lax.dynamic_slice_in_dim(mlp_in_weight, place * cut, cut, axis=0),
        lax.dynamic_slice_in_dim(mlp_out_weight, (place - 8) * cut, cut, axis=0),
    )
    keep, give, send = enter_spatial(core, latents, modulation, piece_t)
    give = after(give, other_qkv, other_out, piece_f)
    parts = [keep, swap(give, 1), swap(send, 2), swap(give, 3)]
    far_t = gather(after(parts[2][2 * latents.shape[0] :], parts[1], parts[3]))

    moved = swap(piece_f, 2)
    back = attend(0, parts, near)
    far_f = gather(after(moved, back[0]))
    back = [(back[0] if d == 0 else swap(back[d], d)) for d in range(4)]
    middle, normed = finish_spatial(core, latents, time_embed, modulation, back)
    other_mlp_in = swap(mlp_in_weight, 1)
    other_mlp_out = swap(mlp_out_weight, 1)

    def regroup(rows):
        rows = rows.reshape(latents.shape)
        return lax.all_to_all(rows, "seq", split_axis=0, concat_axis=0, tiled=True)

    regrouped = regroup(normed)
    partial, rows = attend(1, [regrouped], near)
    far_t = after(far_t, middle, other_mlp_in, other_mlp_out)
    far_other_t = swap(far_t, 1)
    (projected,) = attend(1, [rows], (far_t, far_other_t), [partial])
    projected = regroup(projected)
    far_f = after(far_f, projected)
    far_other_f = swap(far_f, 1)
    rows = latents.shape[0] * latents.shape[1]
    base = jax.ShapeDtypeStruct((rows, width), F32)
    x = jax.ShapeDtypeStruct((rows, width), BF)
    early = (mlp_in_weight, mlp_out_weight, other_mlp_in, other_mlp_out)
    base, x = mlp(True, modulation, (middle, projected), early, (far_f,), [base, x])
    result = jax.ShapeDtypeStruct(latents.shape, F32)
    return mlp(False, modulation, (x, base), (), (far_other_f,), [result])[0]


def solution(mesh):
    in_specs = (
        P("tp", "seq", None),
        P("seq", None),
        P(),
        P(None, None, None, "tp"),
        P(None, "tp", None),
        P(None, "tp"),
        P("tp", None),
    )
    out_specs = P("tp", "seq", None)
    return jax.shard_map(
        on_device, mesh=mesh, in_specs=in_specs, out_specs=out_specs, check_vma=False
    )
```
